32 devices in a mesh: seq: 16 (over z, y, x), tp: 2 (over core).
Axes of the slice: x: 2, y: 2, z: 4, core: 2. Of those that a mesh axis runs over, the one named last changes fastest.
Arguments:
- queries: bfloat16 [16, 4, 8192], P('seq', None, 'tp'), may hold values from -40 to 40
- new_keys: bfloat16 [16, 4, 1024], P('seq', None, 'tp'), may hold values from -6 to 6
- new_values: bfloat16 [16, 4, 1024], P('seq', None, 'tp'), may hold values from -6 to 6
- prefix_keys: bfloat16 [8, 3072, 1024], P(None, 'seq', 'tp'), may hold values from -8 to 8
- prefix_values: bfloat16 [8, 3072, 1024], P(None, 'seq', 'tp'), may hold values from -6 to 6
- page_keys: bfloat16 [256, 64, 1024], P('seq', None, 'tp'), may hold values from -6 to 6
- page_values: bfloat16 [256, 64, 1024], P('seq', None, 'tp'), may hold values from -6 to 6
- out_weight: bfloat16 [8192, 8192], P('tp', 'seq'), may hold values from -0.5 to 0.5
- group_of: int32 [16], replicated, may hold values from 0 to 7, as said below
- prefix_len: int32 [8], replicated, may hold values from 2 to 3072, as said below
- total_len: int32 [16], replicated, may hold values from 3 to 7168, as said below
- page_owner: int32 [256], P('seq'), may hold values from 0 to 15, as said below
- page_slot: int32 [256], P('seq'), may hold values from 0 to 63, as said below
- new_valid: int32 [16, 4], replicated, may hold values from 0 to 1, as said below
Outputs:
- attn_out: bfloat16 [64, 8192], P('tp', 'seq')
The draws below stay inside these ranges and needn't reach their ends.
Inputs may be any that keep to these rules, and one draw needn't show every extreme that they name: `group_of`: every one of the 8 groups has at least one request. `prefix_len`: some group's prefix holds exactly 3072 tokens. `page_owner`: every request owns at least one page and at most 64 pages; one request owns exactly 64. `page_slot`: the pages of one request carry the slots 0, 1, 2 and so on, each once. A request's pages are full except the one of its highest slot, which holds 1 to 64 tokens; total_len is its group's prefix length plus these tokens. `new_valid`: each row is a run of ones followed by zeros, and its first entry is one.
All inputs are finite; a program needn't handle non-finite values.
Results may differ from the reference program's by a relative error of at most 0.022.
Values may be sent and summed in bfloat16 or wider, within the bound.
A program may use at most 192 MiB of HBM per device.

```python
import jax
import jax.numpy as jnp
from jax import lax

D = 8192
HEADS = 64
KV_HEADS = 8
HEAD_DIM = 128
HPK = 8
GROUPS = 8
NEW = 4
PAGE = 64
PAGE_DEV = 16
REQS = 16
PREFIX = 3072
PAGES = 256
N_SEQ = 16


def request_order(key):
    return jax.random.permutation(jax.random.fold_in(key, 107), REQS).astype(jnp.int32)


def group_ids(key):
    folded = jax.random.fold_in(key, 101)
    key_extra, key_order = jax.random.split(folded)
    request_ids = jnp.arange(REQS, dtype=jnp.int32)
    extras = jax.random.randint(key_extra, (REQS,), 0, GROUPS)
    base_ids = jnp.where(request_ids < GROUPS, request_ids % GROUPS, extras)
    ordering = jax.random.permutation(key_order, REQS)
    return base_ids[ordering].astype(jnp.int32)


def prefix_lengths(key):
    folded = jax.random.fold_in(key, 103)
    lengths = jax.random.randint(folded, (GROUPS,), 2, PREFIX + 1)
    longest = group_ids(key)[request_order(key)[0]]
    return jnp.where(jnp.arange(GROUPS, dtype=jnp.int32) == longest, PREFIX, lengths).astype(jnp.int32)


def page_table(key):
    folded = jax.random.fold_in(key, 104)
    key_shuffle, key_tail = jax.random.split(folded)
    order = request_order(key)
    heavy_pages = min(4 * (PAGES // REQS), PAGES - REQS + 1)
    page_ids = jnp.arange(PAGES, dtype=jnp.int32)
    others = 1 + jnp.maximum(page_ids - heavy_pages, 0) % (REQS - 1)
    position = jnp.where(page_ids < heavy_pages, 0, others)
    owners = order[position]
    owners = owners[jax.random.permutation(key_shuffle, PAGES)].astype(jnp.int32)
    one_hot = (owners[:, None] == jnp.arange(REQS, dtype=jnp.int32)[None, :]).astype(jnp.int32)
    earlier = jnp.cumsum(one_hot, axis=0) - one_hot
    slot_ids = jnp.sum(earlier * one_hot, axis=1).astype(jnp.int32)
    counts = jnp.sum(one_hot, axis=0)
    tails = jax.random.randint(key_tail, (REQS,), 1, PAGE + 1)
    tails = jnp.where(jnp.arange(REQS, dtype=jnp.int32) == order[0], PAGE, tails)
    suffix = ((counts - 1) * PAGE + tails).astype(jnp.int32)
    return (owners, slot_ids, suffix)


def draw_group_of(key, part):
    return group_ids(key)


def draw_prefix_len(key, part):
    return prefix_lengths(key)


def draw_total_len(key, part):
    return (prefix_lengths(key)[group_ids(key)] + page_table(key)[2]).astype(jnp.int32)


def draw_page_owner(key, part):
    return page_table(key)[0]


def draw_page_slot(key, part):
    return page_table(key)[1]


def draw_new_valid(key, part):
    counts = jax.random.randint(jax.random.fold_in(key, 105), (REQS,), 1, NEW + 1)
    return (jnp.arange(NEW, dtype=jnp.int32)[None, :] < counts[:, None]).astype(jnp.int32)


def draw_queries(key, part):
    key_main = jax.random.fold_in(jax.random.fold_in(key, 1), 0)
    full_shape = (REQS, NEW, HEADS, HEAD_DIM)
    base = jax.random.normal(key_main, full_shape, jnp.float32)
    return base.reshape(REQS, NEW, HEADS * HEAD_DIM).astype(jnp.bfloat16)


def draw_prefix_keys(key, part):
    key_main = jax.random.fold_in(jax.random.fold_in(key, 2), 0)
    full_shape = (GROUPS, PREFIX, KV_HEADS, HEAD_DIM)
    base = jax.random.normal(key_main, full_shape, jnp.float32)
    return base.reshape(GROUPS, PREFIX, KV_HEADS * HEAD_DIM).astype(jnp.bfloat16)


def shard_levels(stream_key, extent, cuts, smallest, high):
    def one(dim, parts):
        steps = jax.random.uniform(jax.random.fold_in(jax.random.fold_in(stream_key, 6), dim), (parts,), jnp.float32, smallest / len(cuts), high / len(cuts))
        return jnp.repeat(jnp.exp(steps), extent[dim] // parts).reshape((-1,) + (1,) * (len(extent) - dim - 1))

    gain = one(*cuts[0])
    for cut in cuts[1:]:
        gain = gain * one(*cut)
    return gain


def centred(own_key, extent, width, limit, shards=(), kind=jnp.bfloat16):
    entries = width * jax.random.normal(own_key, extent, jnp.float32)
    if shards:
        entries = entries * shard_levels(own_key, extent, shards, -0.22, 0.18)
    return jnp.clip(entries, -limit, limit).astype(kind)


def setup_inputs(seed: int = 0) -> dict:
    key_of = jax.random.split(jax.random.key(seed), 15)
    queries = draw_queries(jax.random.fold_in(key_of[14], 71), 0)
    new_keys = centred(key_of[1], (REQS, NEW, KV_HEADS * HEAD_DIM), 1.0, 6.0, ((0, 16), (2, 2)))
    new_values = centred(key_of[2], (REQS, NEW, KV_HEADS * HEAD_DIM), 1.0, 6.0, ((0, 16), (2, 2)))
    prefix_keys = draw_prefix_keys(jax.random.fold_in(key_of[14], 71), 0)
    prefix_values = centred(key_of[4], (GROUPS, PREFIX, KV_HEADS * HEAD_DIM), 1.0, 6.0, ((1, 16), (2, 2)))
    page_keys = centred(key_of[5], (PAGES, PAGE, KV_HEADS * HEAD_DIM), 1.0, 6.0, ((0, 16), (2, 2)))
    page_values = centred(key_of[6], (PAGES, PAGE, KV_HEADS * HEAD_DIM), 1.0, 6.0, ((0, 16), (2, 2)))
    out_weight = centred(key_of[7], (HEADS * HEAD_DIM, D), HEAD_DIM ** -0.5, 0.5, ((0, 2), (1, 16)))
    group_of = draw_group_of(jax.random.fold_in(key_of[14], 71), 0)
    prefix_len = draw_prefix_len(jax.random.fold_in(key_of[14], 71), 0)
    total_len = draw_total_len(jax.random.fold_in(key_of[14], 71), 0)
    page_owner = draw_page_owner(jax.random.fold_in(key_of[14], 71), 0)
    page_slot = draw_page_slot(jax.random.fold_in(key_of[14], 71), 0)
    new_valid = draw_new_valid(jax.random.fold_in(key_of[14], 71), 0)
    return dict(queries=queries, new_keys=new_keys, new_values=new_values, prefix_keys=prefix_keys, prefix_values=prefix_values, page_keys=page_keys, page_values=page_values, out_weight=out_weight, group_of=group_of, prefix_len=prefix_len, total_len=total_len, page_owner=page_owner, page_slot=page_slot, new_valid=new_valid)


NEG = -1.0e30


def softmax_part(scores, key_mask):
    masked = jnp.where(key_mask, scores, NEG)
    row_peak = jnp.max(masked, axis=-1)
    weights = jnp.where(key_mask, jnp.exp(masked - row_peak[..., None]), 0.0)
    return row_peak, jnp.sum(weights, axis=-1), weights.astype(jnp.bfloat16)


def combine(first_part, second_part):
    peak_a, total_a, out_a = first_part
    peak_b, total_b, out_b = second_part
    top_peak = jnp.maximum(peak_a, peak_b)
    factor_a = jnp.exp(peak_a - top_peak)
    factor_b = jnp.exp(peak_b - top_peak)
    return (top_peak, total_a * factor_a + total_b * factor_b,
            out_a * factor_a[..., None] + out_b * factor_b[..., None])


def reference(queries, new_keys, new_values, prefix_keys, prefix_values, page_keys, page_values,
              out_weight, group_of, prefix_len, total_len, page_owner, page_slot, new_valid):
    score_scale = HEAD_DIM ** -0.5
    query_all = queries.reshape(REQS, NEW, KV_HEADS, HPK, HEAD_DIM).astype(jnp.float32)
    suffix_len = total_len - prefix_len[group_of]

    def prefix_one(request):
        group_idx = group_of[request]
        key_rows = lax.dynamic_index_in_dim(prefix_keys, group_idx, 0, keepdims=False)
        key_rows = key_rows.reshape(PREFIX, KV_HEADS, HEAD_DIM).astype(jnp.float32)
        value_rows = lax.dynamic_index_in_dim(prefix_values, group_idx, 0, keepdims=False)
        value_rows = value_rows.reshape(PREFIX, KV_HEADS, HEAD_DIM).astype(jnp.float32)
        query_row = lax.dynamic_index_in_dim(query_all, request, 0, keepdims=False)
        scores = jnp.einsum("jkhd,pkd->jkhp", query_row, key_rows) * score_scale
        live_keys = jnp.arange(PREFIX, dtype=jnp.int32) < prefix_len[group_idx]
        row_peak, row_total, weights = softmax_part(scores, live_keys)
        values = jnp.einsum("jkhp,pkd->jkhd", weights.astype(jnp.float32), value_rows)
        return row_peak, row_total, values

    prefix_part = lax.map(prefix_one, jnp.arange(REQS, dtype=jnp.int32))

    key_blocks = page_keys.reshape(N_SEQ, PAGE_DEV, PAGE, KV_HEADS, HEAD_DIM)
    value_blocks = page_values.reshape(N_SEQ, PAGE_DEV, PAGE, KV_HEADS, HEAD_DIM)
    owner_blocks = page_owner.reshape(N_SEQ, PAGE_DEV)
    slot_blocks = page_slot.reshape(N_SEQ, PAGE_DEV)

    def pages_one(page_block):
        key_rows, value_rows, owners, slot_ids = page_block
        page_queries = jnp.take(query_all, owners, axis=0)
        scores = jnp.einsum("pjkhd,pikd->pjkhi", page_queries, key_rows.astype(jnp.float32)) * score_scale
        offsets = slot_ids[:, None] * PAGE + jnp.arange(PAGE, dtype=jnp.int32)[None, :]
        live_keys = offsets < jnp.take(suffix_len, owners)[:, None]
        row_peak, row_total, weights = softmax_part(scores, live_keys[:, None, None, None, :])
        values = jnp.einsum("pjkhi,pikd->pjkhd", weights.astype(jnp.float32), value_rows.astype(jnp.float32))
        return row_peak, row_total, values

    page_peak, page_total, page_out = lax.map(pages_one, (key_blocks, value_blocks, owner_blocks, slot_blocks))
    page_peak = page_peak.reshape(PAGES, NEW, KV_HEADS, HPK)
    page_total = page_total.reshape(PAGES, NEW, KV_HEADS, HPK)
    page_out = page_out.reshape(PAGES, NEW, KV_HEADS, HPK, HEAD_DIM)
    suffix_peak = jnp.maximum(jax.ops.segment_max(page_peak, page_owner, num_segments=REQS), NEG)
    factor = jnp.exp(page_peak - suffix_peak[page_owner])
    suffix_total = jax.ops.segment_sum(page_total * factor, page_owner, num_segments=REQS)
    suffix_out = jax.ops.segment_sum(page_out * factor[..., None], page_owner, num_segments=REQS)
    suffix_part = (suffix_peak, suffix_total, suffix_out)

    keys_new = new_keys.reshape(REQS, NEW, KV_HEADS, HEAD_DIM).astype(jnp.float32)
    values_new = new_values.reshape(REQS, NEW, KV_HEADS, HEAD_DIM).astype(jnp.float32)
    scores = jnp.einsum("rjkhd,rikd->rjkhi", query_all, keys_new) * score_scale
    causal = jnp.arange(NEW, dtype=jnp.int32)[None, :] <= jnp.arange(NEW, dtype=jnp.int32)[:, None]
    key_mask = causal[None, :, None, None, :] & (new_valid[:, None, None, None, :] == 1)
    row_peak, row_total, weights = softmax_part(scores, key_mask)
    new_out = jnp.einsum("rjkhi,rikd->rjkhd", weights.astype(jnp.float32), values_new)
    new_part = (row_peak, row_total, new_out)

    final_peak, final_total, final_out = combine(combine(prefix_part, suffix_part), new_part)
    valid_rows = new_valid.astype(jnp.float32)[:, :, None, None, None]
    attention = (final_out / final_total[..., None] * valid_rows).astype(jnp.bfloat16)
    attention = attention.reshape(REQS * NEW, HEADS * HEAD_DIM)
    return jnp.dot(attention, out_weight, preferred_element_type=jnp.float32).astype(jnp.bfloat16)
```

```python
import functools
import math

import jax
import jax.numpy as jnp
from jax import lax
from jax.experimental import pallas as pl
from jax.experimental.pallas import tpu as pltpu
from jax.sharding import PartitionSpec as P

HEAD_DIM = 128
HPK = 8
GROUPS = 8
NEW = 4
ROWS = HPK * NEW
BLOCK_REQS = 16
CHUNK_REQS = 4
TILE = 128
NEG = -1e30
MESH = pl.DeviceIdType.MESH
F32 = jnp.float32
BF16 = jnp.bfloat16


def kernel(
    cfg,
    group_ref,
    plen_ref,
    tlen_ref,
    owner_ref,
    slot_ref,
    valid_ref,
    q_ref,
    nk_ref,
    nv_ref,
    pk_hbm,
    pv_hbm,
    gk_hbm,
    gv_hbm,
    w_hbm,
    out_ref,
    kall,
    vall,
    wall,
    vt,
    mask,
    tmp,
    qtmp,
    qbuf,
    s_scr,
    osend,
    ssend,
    obuf,
    sbuf,
    asend,
    abuf,
    tsend,
    tbuf,
    load_sem,
    q_send,
    q_recv,
    o_send,
    o_recv,
    s_send,
    s_recv,
    a_send,
    a_recv,
    t_send,
    t_recv,
):
    n, tp, reqs, kvs, pre, pages, page = cfg
    pre_rows, page_rows = GROUPS * pre, pages * page
    cached = pre_rows + page_rows
    keys = cached + TILE
    chunk = 384 if keys % 384 == 0 else TILE
    blocks = reqs // BLOCK_REQS
    brows = BLOCK_REQS * ROWS
    per_kv = reqs // CHUNK_REQS
    combiners = kvs * per_kv
    per_block = BLOCK_REQS // CHUNK_REQS
    me = lax.axis_index("seq")
    core = lax.axis_index("tp")
    all_combine = combiners == n

    loads = [
        pltpu.make_async_copy(src, dst, load_sem.at[i])
        for i, (src, dst) in enumerate(
            (
                (pv_hbm, vall.at[pl.ds(0, pre_rows)]),
                (gv_hbm, vall.at[pl.ds(pre_rows, page_rows)]),
                (pk_hbm, kall.at[pl.ds(0, pre_rows)]),
                (gk_hbm, kall.at[pl.ds(pre_rows, page_rows)]),
                (w_hbm, wall),
            )
        )
    ]
    for load in loads:
        load.start()

    barrier = pltpu.get_barrier_semaphore()

    def greet(k, c):
        pl.semaphore_signal(
            barrier, inc=1, device_id={"seq": lax.rem(me + k, n)}, device_id_type=MESH
        )
        return c

    lax.fori_loop(1, n, greet, 0)
    for k in range(1, tp):
        pl.semaphore_signal(
            barrier, inc=1, device_id={"tp": lax.rem(core + k, tp)}, device_id_type=MESH
        )

    q = q_ref[0].astype(F32)
    for h in range(kvs * HPK):
        qtmp[pl.ds(h * NEW, NEW), :] = q[:, h * HEAD_DIM : (h + 1) * HEAD_DIM]
    qbuf[me] = qtmp[...].reshape(kvs, ROWS, HEAD_DIM).astype(BF16)

    pl.semaphore_wait(barrier, n - 1 + tp - 1)

    def to_seq(src, dst, send, recv, peer):
        return pltpu.make_async_remote_copy(
            src_ref=src,
            dst_ref=dst,
            send_sem=send,
            recv_sem=recv,
            device_id={"seq": peer},
            device_id_type=MESH,
        )

    def q_copy(k, source):
        return to_seq(
            qbuf.at[source], qbuf.at[source], q_send.at[k], q_recv.at[source], lax.rem(me + k, n)
        )

    def q_start(k, c):
        q_copy(k, me).start()
        return c

    lax.fori_loop(1, n, q_start, 0)

    lane = lax.broadcasted_iota(jnp.int32, (1, TILE), 1)
    group_vec = jnp.full((1, TILE), -1, jnp.int32)
    total_vec = jnp.zeros((1, TILE), jnp.int32)
    for r in range(reqs):
        group_vec = jnp.where(lane == r, group_ref[r], group_vec)
        total_vec = jnp.where(lane == r, tlen_ref[r], total_vec)
    own_pre = jnp.zeros((1, TILE), jnp.int32)
    for g in range(GROUPS):
        own_pre = jnp.where(group_vec == g, plen_ref[g], own_pre)
    suffix_vec = total_vec - own_pre
    lane_pre = lax.broadcasted_iota(jnp.int32, (pre, TILE), 1)
    pos = me * pre + lax.broadcasted_iota(jnp.int32, (pre, TILE), 0)
    for g in range(GROUPS):
        limit = jnp.where(group_vec == g, plen_ref[g], 0)
        dead = (pos >= limit) & (lane_pre < reqs)
        mask[pl.ds(g * pre, pre), :] = jnp.where(dead, NEG, 0.0).astype(BF16)
    lane_page = lax.broadcasted_iota(jnp.int32, (page, TILE), 1)
    offset = lax.broadcasted_iota(jnp.int32, (page, TILE), 0)
    for p in range(pages):
        limit = jnp.where(lane == owner_ref[p], suffix_vec, 0)
        dead = (offset + slot_ref[p] * page >= limit) & (lane_page < reqs)
        mask[pl.ds(pre_rows + p * page, page), :] = jnp.where(dead, NEG, 0.0).astype(BF16)
    lane_new = lax.broadcasted_iota(jnp.int32, (TILE, TILE), 1)
    row_new = lax.broadcasted_iota(jnp.int32, (TILE, TILE), 0)
    valid_rows = jnp.zeros((TILE, TILE), jnp.int32)
    for i in range(NEW):
        valid_rows = jnp.where(row_new == i, valid_ref[me, i], valid_rows)
    alive = (
        (valid_rows == 1)
        & ((lane_new == me) | ((lane_new >= reqs) & (row_new <= lane_new - reqs)))
        & (row_new < NEW)
    )
    mask[pl.ds(cached, TILE), :] = jnp.where(alive, 0.0, NEG).astype(BF16)

    for new_ref, all_ref in ((nk_ref, kall), (nv_ref, vall)):
        tmp[...] = jnp.zeros_like(tmp)
        tmp[pl.ds(0, NEW), :] = new_ref[0].astype(F32)
        all_ref[pl.ds(cached, 16), :] = tmp[...].astype(BF16)
        all_ref[pl.ds(cached + 16, TILE - 16), :] = jnp.zeros((TILE - 16, kvs * HEAD_DIM), BF16)

    loads[0].wait()
    loads[1].wait()
    for kv in range(kvs):
        vt[kv, pl.ds(HEAD_DIM, 16), :] = jnp.ones((16, keys), BF16)

    def turn(c, carry):
        rows = pl.ds(pl.multiple_of(c * chunk, chunk), chunk)
        for kv in range(kvs):
            vt[kv, pl.ds(0, HEAD_DIM), rows] = vall[rows, kv * HEAD_DIM : (kv + 1) * HEAD_DIM].T
        return carry

    lax.fori_loop(0, keys // chunk, turn, 0)
    loads[2].wait()
    loads[3].wait()

    def q_wait(k, c):
        source = lax.rem(me + n - k, n)
        q_copy(k, source).wait_recv()
        return c

    lax.fori_loop(1, n, q_wait, 0)

    scale = HEAD_DIM ** (-0.5) * math.log2(math.e)

    def o_copy(dest, source):
        return to_seq(
            osend.at[dest], obuf.at[source], o_send.at[dest], o_recv.at[source], dest
        ), to_seq(ssend.at[dest], sbuf.at[source], s_send.at[dest], s_recv.at[source], dest)

    def attend(it, carry):
        kv, rb = it // blocks, it % blocks
        qs = qbuf[pl.ds(rb * BLOCK_REQS, BLOCK_REQS), kv].reshape(brows, HEAD_DIM)
        hot_row = lax.broadcasted_iota(jnp.int32, (brows, TILE), 0)
        hot_lane = lax.broadcasted_iota(jnp.int32, (brows, TILE), 1)
        hot = (hot_lane == rb * BLOCK_REQS + hot_row // ROWS) | (
            hot_lane == reqs + hot_row % NEW
        )
        q_aug = jnp.concatenate([qs, jnp.where(hot, 1.0, 0.0).astype(BF16)], axis=1)
        lanes = pl.ds(pl.multiple_of(kv * HEAD_DIM, HEAD_DIM), HEAD_DIM)

        def score(c, peak):
            rows = pl.ds(pl.multiple_of(c * chunk, chunk), chunk)
            k_aug = jnp.concatenate([kall[rows, lanes], mask[rows, :]], axis=1)
            s = lax.dot_general(
                k_aug, q_aug, (((1,), (1,)), ((), ())), preferred_element_type=F32
            )
            s_scr[rows, :] = s
            return jnp.maximum(peak, jnp.max(s.reshape(chunk // 8, 8, brows), axis=0))

        peak = lax.fori_loop(0, keys // chunk, score, jnp.full((8, brows), 4 * NEG, F32))
        peak = jnp.max(peak, axis=0, keepdims=True) * scale

        def weigh(c, acc):
            rows = pl.ds(pl.multiple_of(c * chunk, chunk), chunk)
            w = jnp.exp2(s_scr[rows, :] * scale - peak).astype(BF16)
            return acc + jnp.dot(vt[kv, :, rows], w, preferred_element_type=F32)

        acc = lax.fori_loop(
            0, keys // chunk, weigh, jnp.zeros((HEAD_DIM + 16, brows), F32)
        )
        row8 = lax.broadcasted_iota(jnp.int32, (8, brows), 0)
        stats = jnp.where(row8 == 0, peak, acc[HEAD_DIM : HEAD_DIM + 8])
        for i in range(per_block):
            dest = it * per_block + i
            cols = slice(i * TILE, (i + 1) * TILE)
            osend[dest] = acc[:HEAD_DIM, cols].astype(BF16)
            ssend[dest] = stats[:, cols]

            @pl.when(dest != me)
            def _():
                for copy in o_copy(dest, me):
                    copy.start()

        return carry

    lax.fori_loop(0, kvs * blocks, attend, 0)

    def a_place(source):
        return abuf.at[source // per_kv, pl.ds((source % per_kv) * CHUNK_REQS * NEW, CHUNK_REQS * NEW)]

    def a_copy(k, source):
        return to_seq(
            asend, a_place(source), a_send.at[k], a_recv.at[source], lax.rem(me + k, n)
        )

    def combine():
        obuf[me] = osend[me]
        sbuf[me] = ssend[me]

        def o_wait(k, c):
            source = lax.rem(me + n - k, n)
            for copy in o_copy(me, source):
                copy.wait_recv()
            return c

        lax.fori_loop(1, n, o_wait, 0)
        stats = sbuf[...]
        peak = stats[:, 0, :]
        factor = jnp.exp2(peak - jnp.max(peak, axis=0, keepdims=True))
        total = jnp.sum(stats[:, 1, :] * factor, axis=0, keepdims=True)
        outs = jnp.zeros((HEAD_DIM, TILE), F32)
        for source in range(n):
            outs = outs + obuf[source].astype(F32) * factor[source : source + 1]
        first = (me % per_kv) * CHUNK_REQS
        real = jnp.zeros((1, TILE), jnp.int32)
        for r in range(CHUNK_REQS):
            for j in range(NEW):
                real = jnp.where(
                    (lane // ROWS == r) & (lane % NEW == j), valid_ref[first + r, j], real
                )
        x = (outs / total * real.astype(F32)).astype(BF16)
        a = lax.broadcasted_iota(jnp.int32, (TILE, TILE), 0)
        b = lax.broadcasted_iota(jnp.int32, (TILE, TILE), 1)
        pick = b == ((a // NEW) % CHUNK_REQS) * ROWS + (a // (CHUNK_REQS * NEW)) * NEW + a % NEW
        y = lax.dot_general(
            jnp.where(pick, 1.0, 0.0).astype(BF16),
            x,
            (((1,), (1,)), ((), ())),
            preferred_element_type=F32,
        ).astype(BF16)
        step = CHUNK_REQS * NEW
        for h in range(HPK):
            asend[:, h * HEAD_DIM : (h + 1) * HEAD_DIM] = y[h * step : (h + 1) * step]
        abuf[me // per_kv, pl.ds((me % per_kv) * step, step), :] = asend[...]

        def a_start(k, c):
            a_copy(k, me).start()
            return c

        lax.fori_loop(1, n, a_start, 0)

    if all_combine:
        combine()
    else:
        pl.when(me < combiners)(combine)

    loads[4].wait()

    def a_wait(source, c):
        @pl.when(source != me)
        def _():
            a_copy(0, source).wait_recv()

        return c

    lax.fori_loop(0, combiners, a_wait, 0)
    width = HPK * HEAD_DIM
    terms = jnp.dot(abuf[0], wall[pl.ds(0, width), :], preferred_element_type=F32)
    for kv in range(1, kvs):
        terms = terms + jnp.dot(
            abuf[kv], wall[pl.ds(kv * width, width), :], preferred_element_type=F32
        )
    rows_out = out_ref.shape[0]
    tsend[...] = terms.reshape(tp, rows_out, terms.shape[1])

    def t_copy(k, peer, source):
        return pltpu.make_async_remote_copy(
            src_ref=tbuf.at[tp + k - 1],
            dst_ref=tbuf.at[source],
            send_sem=t_send.at[k],
            recv_sem=t_recv.at[source],
            device_id={"tp": peer},
            device_id_type=MESH,
        )

    for k in range(1, tp):
        peer = lax.rem(core + k, tp)
        tbuf[tp + k - 1] = tsend[peer].astype(BF16)
        t_copy(k, peer, core).start()
    out = tsend[core]
    for k in range(1, tp):
        source = lax.rem(core + tp - k, tp)
        t_copy(k, source, source).wait_recv()
        out = out + tbuf[source].astype(F32)
    out_ref[...] = out.astype(BF16)

    def q_done(k, c):
        q_copy(k, me).wait_send()
        return c

    lax.fori_loop(1, n, q_done, 0)

    def o_done(dest, c):
        @pl.when(dest != me)
        def _():
            for copy in o_copy(dest, me):
                copy.wait_send()

        return c

    lax.fori_loop(0, combiners, o_done, 0)

    def a_done():
        def one(k, c):
            a_copy(k, me).wait_send()
            return c

        lax.fori_loop(1, n, one, 0)

    if all_combine:
        a_done()
    else:
        pl.when(me < combiners)(a_done)
    for k in range(1, tp):
        t_copy(k, lax.rem(core + k, tp), core).wait_send()


def local(
    n,
    tp,
    queries,
    new_keys,
    new_values,
    prefix_keys,
    prefix_values,
    page_keys,
    page_values,
    out_weight,
    group_of,
    prefix_len,
    total_len,
    page_owner,
    page_slot,
    new_valid,
):
    reqs = group_of.shape[0]
    kvs = new_keys.shape[2] // HEAD_DIM
    pre = prefix_keys.shape[1]
    pages, page = page_keys.shape[:2]
    width = kvs * HEAD_DIM
    keys = GROUPS * pre + pages * page + TILE
    features = out_weight.shape[1]
    combiners = kvs * reqs // CHUNK_REQS
    rows_out = reqs * NEW // tp
    smem = pl.BlockSpec(memory_space=pltpu.SMEM)
    vmem = pl.BlockSpec(memory_space=pltpu.VMEM)
    hbm = pl.BlockSpec(memory_space=pl.ANY)
    dma = pltpu.SemaphoreType.DMA
    return pl.pallas_call(
        functools.partial(kernel, (n, tp, reqs, kvs, pre, pages, page)),
        out_shape=jax.ShapeDtypeStruct((rows_out, features), BF16),
        in_specs=[smem] * 6 + [vmem] * 3 + [hbm] * 5,
        out_specs=vmem,
        scratch_shapes=[
            pltpu.VMEM((keys, width), BF16),
            pltpu.VMEM((keys, width), BF16),
            pltpu.VMEM(out_weight.shape, BF16),
            pltpu.VMEM((kvs, HEAD_DIM + 16, keys), BF16),
            pltpu.VMEM((keys, TILE), BF16),
            pltpu.VMEM((16, width), F32),
            pltpu.VMEM((kvs * ROWS, HEAD_DIM), F32),
            pltpu.VMEM((reqs, kvs, ROWS, HEAD_DIM), BF16),
            pltpu.VMEM((keys, BLOCK_REQS * ROWS), F32),
            pltpu.VMEM((combiners, HEAD_DIM, TILE), BF16),
            pltpu.VMEM((combiners, 8, TILE), F32),
            pltpu.VMEM((n, HEAD_DIM, TILE), BF16),
            pltpu.VMEM((n, 8, TILE), F32),
            pltpu.VMEM((CHUNK_REQS * NEW, HPK * HEAD_DIM), BF16),
            pltpu.VMEM((kvs, reqs * NEW, HPK * HEAD_DIM), BF16),
            pltpu.VMEM((tp, rows_out, features), F32),
            pltpu.VMEM((2 * tp - 1, rows_out, features), BF16),
            dma((5,)),
            dma((n,)),
            dma((n,)),
            dma((combiners,)),
            dma((n,)),
            dma((combiners,)),
            dma((n,)),
            dma((n,)),
            dma((n,)),
            dma((tp,)),
            dma((tp,)),
        ],
        compiler_params=pltpu.CompilerParams(
            collective_id=0, has_side_effects=True, vmem_limit_bytes=48 * 2**20
        ),
    )(
        group_of,
        prefix_len,
        total_len,
        page_owner,
        page_slot,
        new_valid,
        queries,
        new_keys,
        new_values,
        prefix_keys.reshape(GROUPS * pre, width),
        prefix_values.reshape(GROUPS * pre, width),
        page_keys.reshape(pages * page, width),
        page_values.reshape(pages * page, width),
        out_weight,
    )


def solution(mesh):
    placed = (
        P("seq", None, "tp"),
        P("seq", None, "tp"),
        P("seq", None, "tp"),
        P(None, "seq", "tp"),
        P(None, "seq", "tp"),
        P("seq", None, "tp"),
        P("seq", None, "tp"),
        P("tp", "seq"),
        P(),
        P(),
        P(),
        P("seq"),
        P("seq"),
        P(),
    )
    return jax.shard_map(
        functools.partial(local, mesh.shape["seq"], mesh.shape["tp"]),
        mesh=mesh,
        in_specs=placed,
        out_specs=P("tp", "seq"),
        check_vma=False,
    )
```

```python
import functools
import math

import jax
import jax.numpy as jnp
from jax import lax
from jax.experimental import pallas as pl
from jax.experimental.pallas import tpu as pltpu
from jax.sharding import PartitionSpec as P

HEAD_DIM = 128
HPK = 8
GROUPS = 8
NEW = 4
ROWS = HPK * NEW
BLOCK_REQS = 16
CHUNK_REQS = 4
TILE = 128
PLANE = 4
NEG = -1e30
MESH = pl.DeviceIdType.MESH
F32 = jnp.float32
BF16 = jnp.bfloat16


def kernel(
    cfg,
    group_ref,
    plen_ref,
    tlen_ref,
    owner_ref,
    slot_ref,
    valid_ref,
    q_ref,
    nk_ref,
    nv_ref,
    pk_hbm,
    pv_hbm,
    gk_hbm,
    gv_hbm,
    w_hbm,
    out_ref,
    kall,
    vall,
    wall,
    vt,
    mask,
    tmp,
    qtmp,
    qbuf,
    s_scr,
    osend,
    ssend,
    obuf,
    sbuf,
    abuf,
    tsend,
    tbuf,
    load_sem,
    q_send,
    q_recv,
    o_send,
    o_recv,
    s_send,
    s_recv,
    a_send,
    a_recv,
    t_send,
    t_recv,
):
    n, tp, reqs, kvs, pre, pages, page = cfg
    pre_rows, page_rows = GROUPS * pre, pages * page
    cached = pre_rows + page_rows
    keys = cached + TILE
    chunk = 384 if keys % 384 == 0 else TILE
    blocks = reqs // BLOCK_REQS
    brows = BLOCK_REQS * ROWS
    per_kv = reqs // CHUNK_REQS
    combiners = kvs * per_kv
    per_block = BLOCK_REQS // CHUNK_REQS
    me = lax.axis_index("seq")
    core = lax.axis_index("tp")
    all_combine = combiners == n

    loads = [
        pltpu.make_async_copy(src, dst, load_sem.at[i])
        for i, (src, dst) in enumerate(
            (
                (pv_hbm, vall.at[pl.ds(0, pre_rows)]),
                (gv_hbm, vall.at[pl.ds(pre_rows, page_rows)]),
                (pk_hbm, kall.at[pl.ds(0, pre_rows)]),
                (gk_hbm, kall.at[pl.ds(pre_rows, page_rows)]),
                (w_hbm, wall),
            )
        )
    ]
    for load in loads:
        load.start()

    barrier = pltpu.get_barrier_semaphore()

    def greet(k, c):
        pl.semaphore_signal(
            barrier, inc=1, device_id={"seq": lax.rem(me + k, n)}, device_id_type=MESH
        )
        return c

    lax.fori_loop(1, n, greet, 0)
    for k in range(1, tp):
        pl.semaphore_signal(
            barrier, inc=1, device_id={"tp": lax.rem(core + k, tp)}, device_id_type=MESH
        )

    q = q_ref[0].astype(F32)
    for h in range(kvs * HPK):
        qtmp[pl.ds(h * NEW, NEW), :] = q[:, h * HEAD_DIM : (h + 1) * HEAD_DIM]
    qbuf[me] = qtmp[...].reshape(kvs, ROWS, HEAD_DIM).astype(BF16)

    pl.semaphore_wait(barrier, n - 1 + tp - 1)

    def to_seq(src, dst, send, recv, peer):
        return pltpu.make_async_remote_copy(
            src_ref=src,
            dst_ref=dst,
            send_sem=send,
            recv_sem=recv,
            device_id={"seq": peer},
            device_id_type=MESH,
        )

    base, place_in = me // PLANE * PLANE, me % PLANE
    layers = n // PLANE

    def spread(place, send, recv, sources):
        def copy(source, peer, k):
            return to_seq(place(source), place(source), send.at[k], recv.at[source], peer)

        def along(k):
            return copy(me, lax.rem(me + k * PLANE, n), k)

        def within(k, source, p):
            return copy(
                source, base + lax.rem(place_in + p, PLANE), layers + k * (PLANE - 1) + p - 1
            )

        def held(source, act):
            if sources == n:
                act()
            else:
                pl.when(source < sources)(act)

        def above(k):
            return lax.rem(me + n - k * PLANE, n)

        def start():
            for k in range(1, layers):
                along(k).start()
            for p in range(1, PLANE):
                within(0, me, p).start()

        def relay():
            for k in range(1, layers):
                source = above(k)

                def pass_on():
                    copy(source, me, 0).wait_recv()
                    for p in range(1, PLANE):
                        within(k, source, p).start()

                held(source, pass_on)

        def finish():
            for p in range(1, PLANE):
                for k in range(layers):
                    source = lax.rem(base + lax.rem(place_in + p, PLANE) + n - k * PLANE, n)
                    held(source, lambda: copy(source, me, 0).wait_recv())

        def done():
            def own():
                for k in range(1, layers):
                    along(k).wait_send()

            held(me, own)
            for k in range(layers):
                for p in range(1, PLANE):
                    held(above(k), lambda: within(k, above(k), p).wait_send())

        return start, relay, finish, done

    q_start, q_relay, q_finish, q_done = spread(lambda source: qbuf.at[source], q_send, q_recv, n)
    q_start()

    lane = lax.broadcasted_iota(jnp.int32, (1, TILE), 1)
    group_vec = jnp.full((1, TILE), -1, jnp.int32)
    total_vec = jnp.zeros((1, TILE), jnp.int32)
    for r in range(reqs):
        group_vec = jnp.where(lane == r, group_ref[r], group_vec)
        total_vec = jnp.where(lane == r, tlen_ref[r], total_vec)
    own_pre = jnp.zeros((1, TILE), jnp.int32)
    for g in range(GROUPS):
        own_pre = jnp.where(group_vec == g, plen_ref[g], own_pre)
    suffix_vec = total_vec - own_pre
    lane_pre = lax.broadcasted_iota(jnp.int32, (pre, TILE), 1)
    pos = me * pre + lax.broadcasted_iota(jnp.int32, (pre, TILE), 0)
    for g in range(GROUPS):
        limit = jnp.where(group_vec == g, plen_ref[g], 0)
        dead = (pos >= limit) & (lane_pre < reqs)
        mask[pl.ds(g * pre, pre), :] = jnp.where(dead, NEG, 0.0).astype(BF16)
    lane_page = lax.broadcasted_iota(jnp.int32, (page, TILE), 1)
    offset = lax.broadcasted_iota(jnp.int32, (page, TILE), 0)
    for p in range(pages):
        limit = jnp.where(lane == owner_ref[p], suffix_vec, 0)
        dead = (offset + slot_ref[p] * page >= limit) & (lane_page < reqs)
        mask[pl.ds(pre_rows + p * page, page), :] = jnp.where(dead, NEG, 0.0).astype(BF16)
    lane_new = lax.broadcasted_iota(jnp.int32, (TILE, TILE), 1)
    row_new = lax.broadcasted_iota(jnp.int32, (TILE, TILE), 0)
    valid_rows = jnp.zeros((TILE, TILE), jnp.int32)
    for i in range(NEW):
        valid_rows = jnp.where(row_new == i, valid_ref[i, me], valid_rows)
    alive = (
        (valid_rows == 1)
        & ((lane_new == me) | ((lane_new >= reqs) & (row_new <= lane_new - reqs)))
        & (row_new < NEW)
    )
    mask[pl.ds(cached, TILE), :] = jnp.where(alive, 0.0, NEG).astype(BF16)

    q_relay()

    for new_ref, all_ref in ((nk_ref, kall), (nv_ref, vall)):
        tmp[...] = jnp.zeros_like(tmp)
        tmp[pl.ds(0, NEW), :] = new_ref[0].astype(F32)
        all_ref[pl.ds(cached, 16), :] = tmp[...].astype(BF16)
        all_ref[pl.ds(cached + 16, TILE - 16), :] = jnp.zeros((TILE - 16, kvs * HEAD_DIM), BF16)

    loads[0].wait()
    loads[1].wait()
    for kv in range(kvs):
        vt[kv, pl.ds(HEAD_DIM, 16), :] = jnp.ones((16, keys), BF16)

    def turn(c, carry):
        rows = pl.ds(pl.multiple_of(c * chunk, chunk), chunk)
        for kv in range(kvs):
            vt[kv, pl.ds(0, HEAD_DIM), rows] = vall[rows, kv * HEAD_DIM : (kv + 1) * HEAD_DIM].T
        return carry

    lax.fori_loop(0, keys // chunk, turn, 0)
    loads[2].wait()
    loads[3].wait()

    q_finish()

    scale = HEAD_DIM ** (-0.5) * math.log2(math.e)

    def o_copy(dest, source):
        return to_seq(
            osend.at[dest], obuf.at[source], o_send.at[dest], o_recv.at[source], dest
        ), to_seq(ssend.at[dest], sbuf.at[source], s_send.at[dest], s_recv.at[source], dest)

    def attend(turn_idx, carry):
        it = lax.rem(turn_idx + 1 + me // PLANE, kvs * blocks)
        kv, rb = it // blocks, it % blocks
        qs = qbuf[pl.ds(rb * BLOCK_REQS, BLOCK_REQS), kv].reshape(brows, HEAD_DIM)
        hot_row = lax.broadcasted_iota(jnp.int32, (brows, TILE), 0)
        hot_lane = lax.broadcasted_iota(jnp.int32, (brows, TILE), 1)
        hot = (hot_lane == rb * BLOCK_REQS + hot_row // ROWS) | (
            hot_lane == reqs + hot_row % NEW
        )
        q_aug = jnp.concatenate([qs, jnp.where(hot, 1.0, 0.0).astype(BF16)], axis=1)
        lanes = pl.ds(pl.multiple_of(kv * HEAD_DIM, HEAD_DIM), HEAD_DIM)

        def score(c, peak):
            rows = pl.ds(pl.multiple_of(c * chunk, chunk), chunk)
            k_aug = jnp.concatenate([kall[rows, lanes], mask[rows, :]], axis=1)
            s = lax.dot_general(
                k_aug, q_aug, (((1,), (1,)), ((), ())), preferred_element_type=F32
            )
            s_scr[rows, :] = s
            return jnp.maximum(peak, jnp.max(s.reshape(chunk // 8, 8, brows), axis=0))

        peak = lax.fori_loop(0, keys // chunk, score, jnp.full((8, brows), 4 * NEG, F32))
        peak = jnp.max(peak, axis=0, keepdims=True) * scale

        def weigh(c, acc):
            rows = pl.ds(pl.multiple_of(c * chunk, chunk), chunk)
            w = jnp.exp2(s_scr[rows, :] * scale - peak).astype(BF16)
            return acc + jnp.dot(vt[kv, :, rows], w, preferred_element_type=F32)

        acc = lax.fori_loop(
            0, keys // chunk, weigh, jnp.zeros((HEAD_DIM + 16, brows), F32)
        )
        row8 = lax.broadcasted_iota(jnp.int32, (8, brows), 0)
        stats = jnp.where(row8 == 0, peak, acc[HEAD_DIM : HEAD_DIM + 8])
        for i in range(per_block):
            dest = it * per_block + i
            cols = slice(i * TILE, (i + 1) * TILE)
            osend[dest] = acc[:HEAD_DIM, cols].astype(BF16)
            ssend[dest] = stats[:, cols]

            @pl.when(dest != me)
            def _():
                for copy in o_copy(dest, me):
                    copy.start()

        return carry

    lax.fori_loop(0, kvs * blocks, attend, 0)

    def a_place(source):
        return abuf.at[source // per_kv, pl.ds((source % per_kv) * CHUNK_REQS * NEW, CHUNK_REQS * NEW)]

    a_start, a_relay, a_finish, a_done = spread(a_place, a_send, a_recv, combiners)

    def combine():
        obuf[me] = osend[me]
        sbuf[me] = ssend[me]

        def o_wait(k, c):
            source = lax.rem(me + n - k, n)
            for copy in o_copy(me, source):
                copy.wait_recv()
            return c

        lax.fori_loop(1, n, o_wait, 0)
        stats = sbuf[...]
        peak = stats[:, 0, :]
        factor = jnp.exp2(peak - jnp.max(peak, axis=0, keepdims=True))
        total = jnp.sum(stats[:, 1, :] * factor, axis=0, keepdims=True)
        outs = jnp.zeros((HEAD_DIM, TILE), F32)
        for source in range(n):
            outs = outs + obuf[source].astype(F32) * factor[source : source + 1]
        first = (me % per_kv) * CHUNK_REQS
        real = jnp.zeros((1, TILE), jnp.int32)
        for r in range(CHUNK_REQS):
            for j in range(NEW):
                real = jnp.where(
                    (lane // ROWS == r) & (lane % NEW == j), valid_ref[j, first + r], real
                )
        x = (outs / total * real.astype(F32)).astype(BF16)
        a = lax.broadcasted_iota(jnp.int32, (TILE, TILE), 0)
        b = lax.broadcasted_iota(jnp.int32, (TILE, TILE), 1)
        pick = b == ((a // NEW) % CHUNK_REQS) * ROWS + (a // (CHUNK_REQS * NEW)) * NEW + a % NEW
        y = lax.dot_general(
            jnp.where(pick, 1.0, 0.0).astype(BF16),
            x,
            (((1,), (1,)), ((), ())),
            preferred_element_type=F32,
        ).astype(BF16)
        step = CHUNK_REQS * NEW
        rows = pl.ds((me % per_kv) * step, step)
        for h in range(HPK):
            abuf[me // per_kv, rows, h * HEAD_DIM : (h + 1) * HEAD_DIM] = y[
                h * step : (h + 1) * step
            ]
        a_start()

    if all_combine:
        combine()
    else:
        pl.when(me < combiners)(combine)

    a_relay()
    loads[4].wait()
    a_finish()
    width = HPK * HEAD_DIM
    terms = jnp.dot(abuf[0], wall[pl.ds(0, width), :], preferred_element_type=F32)
    for kv in range(1, kvs):
        terms = terms + jnp.dot(
            abuf[kv], wall[pl.ds(kv * width, width), :], preferred_element_type=F32
        )
    rows_out = out_ref.shape[0]
    tsend[...] = terms.reshape(tp, rows_out, terms.shape[1])

    def t_copy(k, peer, source):
        return pltpu.make_async_remote_copy(
            src_ref=tbuf.at[tp + k - 1],
            dst_ref=tbuf.at[source],
            send_sem=t_send.at[k],
            recv_sem=t_recv.at[source],
            device_id={"tp": peer},
            device_id_type=MESH,
        )

    for k in range(1, tp):
        peer = lax.rem(core + k, tp)
        tbuf[tp + k - 1] = tsend[peer].astype(BF16)
        t_copy(k, peer, core).start()
    out = tsend[core]
    for k in range(1, tp):
        source = lax.rem(core + tp - k, tp)
        t_copy(k, source, source).wait_recv()
        out = out + tbuf[source].astype(F32)
    out_ref[...] = out.astype(BF16)

    q_done()

    def o_done(dest, c):
        @pl.when(dest != me)
        def _():
            for copy in o_copy(dest, me):
                copy.wait_send()

        return c

    lax.fori_loop(0, combiners, o_done, 0)

    a_done()
    for k in range(1, tp):
        t_copy(k, lax.rem(core + k, tp), core).wait_send()


def local(
    n,
    tp,
    queries,
    new_keys,
    new_values,
    prefix_keys,
    prefix_values,
    page_keys,
    page_values,
    out_weight,
    group_of,
    prefix_len,
    total_len,
    page_owner,
    page_slot,
    new_valid,
):
    reqs = group_of.shape[0]
    kvs = new_keys.shape[2] // HEAD_DIM
    pre = prefix_keys.shape[1]
    pages, page = page_keys.shape[:2]
    width = kvs * HEAD_DIM
    keys = GROUPS * pre + pages * page + TILE
    features = out_weight.shape[1]
    combiners = kvs * reqs // CHUNK_REQS
    rows_out = reqs * NEW // tp
    smem = pl.BlockSpec(memory_space=pltpu.SMEM)
    vmem = pl.BlockSpec(memory_space=pltpu.VMEM)
    hbm = pl.BlockSpec(memory_space=pltpu.HBM)
    dma = pltpu.SemaphoreType.DMA
    return pl.pallas_call(
        functools.partial(kernel, (n, tp, reqs, kvs, pre, pages, page)),
        out_shape=jax.ShapeDtypeStruct((rows_out, features), BF16),
        in_specs=[smem] * 6 + [vmem] * 3 + [hbm] * 5,
        out_specs=vmem,
        scratch_shapes=[
            pltpu.VMEM((keys, width), BF16),
            pltpu.VMEM((keys, width), BF16),
            pltpu.VMEM(out_weight.shape, BF16),
            pltpu.VMEM((kvs, HEAD_DIM + 16, keys), BF16),
            pltpu.VMEM((keys, TILE), BF16),
            pltpu.VMEM((16, width), F32),
            pltpu.VMEM((kvs * ROWS, HEAD_DIM), F32),
            pltpu.VMEM((reqs, kvs, ROWS, HEAD_DIM), BF16),
            pltpu.VMEM((keys, BLOCK_REQS * ROWS), F32),
            pltpu.VMEM((combiners, HEAD_DIM, TILE), BF16),
            pltpu.VMEM((combiners, 8, TILE), F32),
            pltpu.VMEM((n, HEAD_DIM, TILE), BF16),
            pltpu.VMEM((n, 8, TILE), F32),
            pltpu.VMEM((kvs, reqs * NEW, HPK * HEAD_DIM), BF16),
            pltpu.VMEM((tp, rows_out, features), F32),
            pltpu.VMEM((2 * tp - 1, rows_out, features), BF16),
            dma((5,)),
            dma((n,)),
            dma((n,)),
            dma((combiners,)),
            dma((n,)),
            dma((combiners,)),
            dma((n,)),
            dma((n,)),
            dma((n,)),
            dma((tp,)),
            dma((tp,)),
        ],
        compiler_params=pltpu.CompilerParams(
            collective_id=0, has_side_effects=True, vmem_limit_bytes=63 * 2**20
        ),
    )(
        group_of,
        prefix_len,
        total_len,
        page_owner,
        page_slot,
        new_valid.T,
        queries,
        new_keys,
        new_values,
        prefix_keys.reshape(GROUPS * pre, width),
        prefix_values.reshape(GROUPS * pre, width),
        page_keys.reshape(pages * page, width),
        page_values.reshape(pages * page, width),
        out_weight,
    )


def solution(mesh):
    placed = (
        P("seq", None, "tp"),
        P("seq", None, "tp"),
        P("seq", None, "tp"),
        P(None, "seq", "tp"),
        P(None, "seq", "tp"),
        P("seq", None, "tp"),
        P("seq", None, "tp"),
        P("tp", "seq"),
        P(),
        P(),
        P(),
        P("seq"),
        P("seq"),
        P(),
    )
    return jax.shard_map(
        functools.partial(local, mesh.shape["seq"], mesh.shape["tp"]),
        mesh=mesh,
        in_specs=placed,
        out_specs=P("tp", "seq"),
        check_vma=False,
    )
```

```python
import functools
import math

import jax
import jax.numpy as jnp
from jax import lax
from jax.experimental import pallas as pl
from jax.experimental.pallas import tpu as pltpu
from jax.sharding import PartitionSpec as P

HEAD_DIM = 128
HPK = 8
GROUPS = 8
NEW = 4
ROWS = HPK * NEW
BLOCK_REQS = 16
CHUNK_REQS = 4
TILE = 128
PLANE = 4
NEG = -1e30
MESH = pl.DeviceIdType.MESH
F32 = jnp.float32
BF16 = jnp.bfloat16


def kernel(
    cfg,
    group_ref,
    plen_ref,
    tlen_ref,
    owner_ref,
    slot_ref,
    valid_ref,
    q_ref,
    nk_ref,
    nv_ref,
    pk_hbm,
    pv_hbm,
    gk_hbm,
    gv_hbm,
    w_hbm,
    out_ref,
    kall,
    vall,
    wall,
    vt,
    mask,
    tmp,
    qtmp,
    qbuf,
    s_scr,
    osend,
    ssend,
    obuf,
    sbuf,
    abuf,
    tsend,
    tbuf,
    load_sem,
    q_send,
    q_recv,
    o_send,
    o_recv,
    s_send,
    s_recv,
    a_send,
    a_recv,
    t_send,
    t_recv,
):
    n, tp, reqs, kvs, pre, pages, page = cfg
    pre_rows, page_rows = GROUPS * pre, pages * page
    cached = pre_rows + page_rows
    keys = cached + TILE
    chunk = 896 if keys % 896 == 0 else TILE
    blocks = reqs // BLOCK_REQS
    brows = BLOCK_REQS * ROWS
    per_kv = reqs // CHUNK_REQS
    combiners = kvs * per_kv
    per_block = BLOCK_REQS // CHUNK_REQS
    me = lax.axis_index("seq")
    core = lax.axis_index("tp")
    all_combine = combiners == n

    loads = [
        pltpu.make_async_copy(src, dst, load_sem.at[i])
        for i, (src, dst) in enumerate(
            (
                (pv_hbm, vall.at[pl.ds(0, pre_rows)]),
                (gv_hbm, vall.at[pl.ds(pre_rows, page_rows)]),
                (pk_hbm, kall.at[pl.ds(0, pre_rows)]),
                (gk_hbm, kall.at[pl.ds(pre_rows, page_rows)]),
                (w_hbm, wall),
            )
        )
    ]
    for load in loads:
        load.start()

    barrier = pltpu.get_barrier_semaphore()

    def greet(k, c):
        pl.semaphore_signal(
            barrier, inc=1, device_id={"seq": lax.rem(me + k, n)}, device_id_type=MESH
        )
        return c

    lax.fori_loop(1, n, greet, 0)
    for k in range(1, tp):
        pl.semaphore_signal(
            barrier, inc=1, device_id={"tp": lax.rem(core + k, tp)}, device_id_type=MESH
        )

    q = q_ref[0].astype(F32)
    for h in range(kvs * HPK):
        qtmp[pl.ds(h * NEW, NEW), :] = q[:, h * HEAD_DIM : (h + 1) * HEAD_DIM]
    qbuf[me] = qtmp[...].reshape(kvs, ROWS, HEAD_DIM).astype(BF16)

    pl.semaphore_wait(barrier, n - 1 + tp - 1)

    def to_seq(src, dst, send, recv, peer):
        return pltpu.make_async_remote_copy(
            src_ref=src,
            dst_ref=dst,
            send_sem=send,
            recv_sem=recv,
            device_id={"seq": peer},
            device_id_type=MESH,
        )

    base, place_in = me // PLANE * PLANE, me % PLANE
    layers = n // PLANE

    def spread(place, send, recv, sources):
        def copy(source, peer, k):
            return to_seq(place(source), place(source), send.at[k], recv.at[source], peer)

        def along(k):
            return copy(me, lax.rem(me + k * PLANE, n), k)

        def within(k, source, p):
            return copy(
                source, base + lax.rem(place_in + p, PLANE), layers + k * (PLANE - 1) + p - 1
            )

        def held(source, act):
            if sources == n:
                act()
            else:
                pl.when(source < sources)(act)

        def above(k):
            return lax.rem(me + n - k * PLANE, n)

        def start():
            for k in range(1, layers):
                along(k).start()
            for p in range(1, PLANE):
                within(0, me, p).start()

        def relay():
            for k in range(1, layers):
                source = above(k)

                def pass_on():
                    copy(source, me, 0).wait_recv()
                    for p in range(1, PLANE):
                        within(k, source, p).start()

                held(source, pass_on)

        def finish():
            for p in range(1, PLANE):
                for k in range(layers):
                    source = lax.rem(base + lax.rem(place_in + p, PLANE) + n - k * PLANE, n)
                    held(source, lambda: copy(source, me, 0).wait_recv())

        def done():
            def own():
                for k in range(1, layers):
                    along(k).wait_send()

            held(me, own)
            for k in range(layers):
                for p in range(1, PLANE):
                    held(above(k), lambda: within(k, above(k), p).wait_send())

        return start, relay, finish, done

    q_start, q_relay, q_finish, q_done = spread(lambda source: qbuf.at[source], q_send, q_recv, n)
    q_start()

    lane = lax.broadcasted_iota(jnp.int32, (1, TILE), 1)
    group_vec = jnp.full((1, TILE), -1, jnp.int32)
    total_vec = jnp.zeros((1, TILE), jnp.int32)
    for r in range(reqs):
        group_vec = jnp.where(lane == r, group_ref[r], group_vec)
        total_vec = jnp.where(lane == r, tlen_ref[r], total_vec)
    own_pre = jnp.zeros((1, TILE), jnp.int32)
    for g in range(GROUPS):
        own_pre = jnp.where(group_vec == g, plen_ref[g], own_pre)
    suffix_vec = total_vec - own_pre
    lane_pre = lax.broadcasted_iota(jnp.int32, (pre, TILE), 1)
    pos = me * pre + lax.broadcasted_iota(jnp.int32, (pre, TILE), 0)
    for g in range(GROUPS):
        limit = jnp.where(group_vec == g, plen_ref[g], 0)
        dead = (pos >= limit) & (lane_pre < reqs)
        mask[pl.ds(g * pre, pre), :] = jnp.where(dead, NEG, 0.0).astype(BF16)
    lane_page = lax.broadcasted_iota(jnp.int32, (page, TILE), 1)
    offset = lax.broadcasted_iota(jnp.int32, (page, TILE), 0)
    for p in range(pages):
        limit = jnp.where(lane == owner_ref[p], suffix_vec, 0)
        dead = (offset + slot_ref[p] * page >= limit) & (lane_page < reqs)
        mask[pl.ds(pre_rows + p * page, page), :] = jnp.where(dead, NEG, 0.0).astype(BF16)
    lane_new = lax.broadcasted_iota(jnp.int32, (TILE, TILE), 1)
    row_new = lax.broadcasted_iota(jnp.int32, (TILE, TILE), 0)
    valid_rows = jnp.zeros((TILE, TILE), jnp.int32)
    for i in range(NEW):
        valid_rows = jnp.where(row_new == i, valid_ref[i, me], valid_rows)
    alive = (
        (valid_rows == 1)
        & ((lane_new == me) | ((lane_new >= reqs) & (row_new <= lane_new - reqs)))
        & (row_new < NEW)
    )
    mask[pl.ds(cached, TILE), :] = jnp.where(alive, 0.0, NEG).astype(BF16)

    q_relay()

    for new_ref, all_ref in ((nk_ref, kall), (nv_ref, vall)):
        tmp[...] = jnp.zeros_like(tmp)
        tmp[pl.ds(0, NEW), :] = new_ref[0].astype(F32)
        all_ref[pl.ds(cached, 16), :] = tmp[...].astype(BF16)
        all_ref[pl.ds(cached + 16, TILE - 16), :] = jnp.zeros((TILE - 16, kvs * HEAD_DIM), BF16)

    loads[0].wait()
    loads[1].wait()
    for kv in range(kvs):
        vt[kv, pl.ds(HEAD_DIM, 16), :] = jnp.ones((16, keys), BF16)

    def turn(c, carry):
        rows = pl.ds(pl.multiple_of(c * chunk, chunk), chunk)
        for kv in range(kvs):
            vt[kv, pl.ds(0, HEAD_DIM), rows] = vall[rows, kv * HEAD_DIM : (kv + 1) * HEAD_DIM].T
        return carry

    lax.fori_loop(0, keys // chunk, turn, 0)
    loads[2].wait()
    loads[3].wait()

    q_finish()

    scale = HEAD_DIM ** (-0.5) * math.log2(math.e)

    def o_copy(dest, source):
        return to_seq(
            osend.at[dest], obuf.at[source], o_send.at[dest], o_recv.at[source], dest
        ), to_seq(ssend.at[dest], sbuf.at[source], s_send.at[dest], s_recv.at[source], dest)

    def attend(turn_idx, carry):
        it = lax.rem(turn_idx + 1 + me // PLANE, kvs * blocks)
        kv, rb = it // blocks, it % blocks
        qs = qbuf[pl.ds(rb * BLOCK_REQS, BLOCK_REQS), kv].reshape(brows, HEAD_DIM)
        hot_row = lax.broadcasted_iota(jnp.int32, (brows, TILE), 0)
        hot_lane = lax.broadcasted_iota(jnp.int32, (brows, TILE), 1)
        hot = (hot_lane == rb * BLOCK_REQS + hot_row // ROWS) | (
            hot_lane == reqs + hot_row % NEW
        )
        q_aug = jnp.concatenate([qs, jnp.where(hot, 1.0, 0.0).astype(BF16)], axis=1)
        lanes = pl.ds(pl.multiple_of(kv * HEAD_DIM, HEAD_DIM), HEAD_DIM)

        def score(c, peak):
            rows = pl.ds(pl.multiple_of(c * chunk, chunk), chunk)
            k_aug = jnp.concatenate([kall[rows, lanes], mask[rows, :]], axis=1)
            s = lax.dot_general(
                k_aug, q_aug, (((1,), (1,)), ((), ())), preferred_element_type=F32
            )
            s_scr[rows, :] = s
            return jnp.maximum(peak, jnp.max(s.reshape(chunk // 8, 8, brows), axis=0))

        peak = lax.fori_loop(0, keys // chunk, score, jnp.full((8, brows), 4 * NEG, F32), unroll=True)
        peak = jnp.max(peak, axis=0, keepdims=True) * scale

        def weigh(c, acc):
            rows = pl.ds(pl.multiple_of(c * chunk, chunk), chunk)
            w = jnp.exp2(s_scr[rows, :] * scale - peak).astype(BF16)
            return acc + jnp.dot(vt[kv, :, rows], w, preferred_element_type=F32)

        acc = lax.fori_loop(
            0, keys // chunk, weigh, jnp.zeros((HEAD_DIM + 16, brows), F32), unroll=True
        )
        row8 = lax.broadcasted_iota(jnp.int32, (8, brows), 0)
        stats = jnp.where(row8 == 0, peak, acc[HEAD_DIM : HEAD_DIM + 8])
        for i in range(per_block):
            dest = it * per_block + i
            cols = slice(i * TILE, (i + 1) * TILE)
            osend[dest] = acc[:HEAD_DIM, cols].astype(BF16)
            ssend[dest] = stats[:, cols]

            @pl.when(dest != me)
            def _():
                for copy in o_copy(dest, me):
                    copy.start()

        return carry

    lax.fori_loop(0, kvs * blocks, attend, 0)

    def a_place(source):
        return abuf.at[source // per_kv, pl.ds((source % per_kv) * CHUNK_REQS * NEW, CHUNK_REQS * NEW)]

    a_start, a_relay, a_finish, a_done = spread(a_place, a_send, a_recv, combiners)

    def combine():
        obuf[me] = osend[me]
        sbuf[me] = ssend[me]

        def o_wait(k, c):
            source = lax.rem(me + n - k, n)
            for copy in o_copy(me, source):
                copy.wait_recv()
            return c

        lax.fori_loop(1, n, o_wait, 0)
        stats = sbuf[...]
        peak = stats[:, 0, :]
        factor = jnp.exp2(peak - jnp.max(peak, axis=0, keepdims=True))
        total = jnp.sum(stats[:, 1, :] * factor, axis=0, keepdims=True)
        outs = jnp.zeros((HEAD_DIM, TILE), F32)
        for source in range(n):
            outs = outs + obuf[source].astype(F32) * factor[source : source + 1]
        first = (me % per_kv) * CHUNK_REQS
        real = jnp.zeros((1, TILE), jnp.int32)
        for r in range(CHUNK_REQS):
            for j in range(NEW):
                real = jnp.where(
                    (lane // ROWS == r) & (lane % NEW == j), valid_ref[j, first + r], real
                )
        x = (outs / total * real.astype(F32)).astype(BF16)
        a = lax.broadcasted_iota(jnp.int32, (TILE, TILE), 0)
        b = lax.broadcasted_iota(jnp.int32, (TILE, TILE), 1)
        pick = b == ((a // NEW) % CHUNK_REQS) * ROWS + (a // (CHUNK_REQS * NEW)) * NEW + a % NEW
        y = lax.dot_general(
            jnp.where(pick, 1.0, 0.0).astype(BF16),
            x,
            (((1,), (1,)), ((), ())),
            preferred_element_type=F32,
        ).astype(BF16)
        step = CHUNK_REQS * NEW
        rows = pl.ds((me % per_kv) * step, step)
        for h in range(HPK):
            abuf[me // per_kv, rows, h * HEAD_DIM : (h + 1) * HEAD_DIM] = y[
                h * step : (h + 1) * step
            ]
        a_start()

    if all_combine:
        combine()
    else:
        pl.when(me < combiners)(combine)

    a_relay()
    loads[4].wait()
    a_finish()
    width = HPK * HEAD_DIM
    terms = jnp.dot(abuf[0], wall[pl.ds(0, width), :], preferred_element_type=F32)
    for kv in range(1, kvs):
        terms = terms + jnp.dot(
            abuf[kv], wall[pl.ds(kv * width, width), :], preferred_element_type=F32
        )
    rows_out = out_ref.shape[0]
    tsend[...] = terms.reshape(tp, rows_out, terms.shape[1])

    def t_copy(k, peer, source):
        return pltpu.make_async_remote_copy(
            src_ref=tbuf.at[tp + k - 1],
            dst_ref=tbuf.at[source],
            send_sem=t_send.at[k],
            recv_sem=t_recv.at[source],
            device_id={"tp": peer},
            device_id_type=MESH,
        )

    for k in range(1, tp):
        peer = lax.rem(core + k, tp)
        tbuf[tp + k - 1] = tsend[peer].astype(BF16)
        t_copy(k, peer, core).start()
    out = tsend[core]
    for k in range(1, tp):
        source = lax.rem(core + tp - k, tp)
        t_copy(k, source, source).wait_recv()
        out = out + tbuf[source].astype(F32)
    out_ref[...] = out.astype(BF16)

    q_done()

    def o_done(dest, c):
        @pl.when(dest != me)
        def _():
            for copy in o_copy(dest, me):
                copy.wait_send()

        return c

    lax.fori_loop(0, combiners, o_done, 0)

    a_done()
    for k in range(1, tp):
        t_copy(k, lax.rem(core + k, tp), core).wait_send()


def local(
    n,
    tp,
    queries,
    new_keys,
    new_values,
    prefix_keys,
    prefix_values,
    page_keys,
    page_values,
    out_weight,
    group_of,
    prefix_len,
    total_len,
    page_owner,
    page_slot,
    new_valid,
):
    reqs = group_of.shape[0]
    kvs = new_keys.shape[2] // HEAD_DIM
    pre = prefix_keys.shape[1]
    pages, page = page_keys.shape[:2]
    width = kvs * HEAD_DIM
    keys = GROUPS * pre + pages * page + TILE
    features = out_weight.shape[1]
    combiners = kvs * reqs // CHUNK_REQS
    rows_out = reqs * NEW // tp
    smem = pl.BlockSpec(memory_space=pltpu.SMEM)
    vmem = pl.BlockSpec(memory_space=pltpu.VMEM)
    hbm = pl.BlockSpec(memory_space=pltpu.HBM)
    dma = pltpu.SemaphoreType.DMA
    return pl.pallas_call(
        functools.partial(kernel, (n, tp, reqs, kvs, pre, pages, page)),
        out_shape=jax.ShapeDtypeStruct((rows_out, features), BF16),
        in_specs=[smem] * 6 + [vmem] * 3 + [hbm] * 5,
        out_specs=vmem,
        scratch_shapes=[
            pltpu.VMEM((keys, width), BF16),
            pltpu.VMEM((keys, width), BF16),
            pltpu.VMEM(out_weight.shape, BF16),
            pltpu.VMEM((kvs, HEAD_DIM + 16, keys), BF16),
            pltpu.VMEM((keys, TILE), BF16),
            pltpu.VMEM((16, width), F32),
            pltpu.VMEM((kvs * ROWS, HEAD_DIM), F32),
            pltpu.VMEM((reqs, kvs, ROWS, HEAD_DIM), BF16),
            pltpu.VMEM((keys, BLOCK_REQS * ROWS), F32),
            pltpu.VMEM((combiners, HEAD_DIM, TILE), BF16),
            pltpu.VMEM((combiners, 8, TILE), F32),
            pltpu.VMEM((n, HEAD_DIM, TILE), BF16),
            pltpu.VMEM((n, 8, TILE), F32),
            pltpu.VMEM((kvs, reqs * NEW, HPK * HEAD_DIM), BF16),
            pltpu.VMEM((tp, rows_out, features), F32),
            pltpu.VMEM((2 * tp - 1, rows_out, features), BF16),
            dma((5,)),
            dma((n,)),
            dma((n,)),
            dma((combiners,)),
            dma((n,)),
            dma((combiners,)),
            dma((n,)),
            dma((n,)),
            dma((n,)),
            dma((tp,)),
            dma((tp,)),
        ],
        compiler_params=pltpu.CompilerParams(
            collective_id=0, has_side_effects=True, vmem_limit_bytes=63 * 2**20
        ),
    )(
        group_of,
        prefix_len,
        total_len,
        page_owner,
        page_slot,
        new_valid.T,
        queries,
        new_keys,
        new_values,
        prefix_keys.reshape(GROUPS * pre, width),
        prefix_values.reshape(GROUPS * pre, width),
        page_keys.reshape(pages * page, width),
        page_values.reshape(pages * page, width),
        out_weight,
    )


def solution(mesh):
    placed = (
        P("seq", None, "tp"),
        P("seq", None, "tp"),
        P("seq", None, "tp"),
        P(None, "seq", "tp"),
        P(None, "seq", "tp"),
        P("seq", None, "tp"),
        P("seq", None, "tp"),
        P("tp", "seq"),
        P(),
        P(),
        P(),
        P("seq"),
        P("seq"),
        P(),
    )
    return jax.shard_map(
        functools.partial(local, mesh.shape["seq"], mesh.shape["tp"]),
        mesh=mesh,
        in_specs=placed,
        out_specs=P("tp", "seq"),
        check_vma=False,
    )
```
